256 devices in a mesh: grp: 32 (over z, y), mem: 8 (over x, core).
Axes of the slice: x: 4, y: 4, z: 8, core: 2. Of those that a mesh axis runs over, the one named last changes fastest.
Arguments:
- tokens: bfloat16 [4096, 3584], P(('grp', 'mem')), may hold values from -6 to 6
- expert_ids: int32 [4096, 8], P(('grp', 'mem')), may hold values from 0 to 127, as said below
- gates: float32 [4096, 8], P(('grp', 'mem')), may hold values from 0.1 to 0.6
- gate_weight: bfloat16 [256, 3584, 512], P(('grp', 'mem')), may hold values from -0.09375 to 0.09375
- up_weight: bfloat16 [256, 3584, 512], P(('grp', 'mem')), may hold values from -0.09375 to 0.09375
- down_weight: bfloat16 [256, 512, 3584], P(('grp', 'mem')), may hold values from -0.1875 to 0.1875
Outputs:
- mixed: bfloat16 [4096, 3584], P(('grp', 'mem'))
The draws below stay inside these ranges and needn't reach their ends.
Inputs may be any that keep to these rules, and one draw needn't show every extreme that they name: `expert_ids`: each row names 8 different experts, all within at most 4 of the 8 groups of 16 consecutive experts. The rows of one device (aligned blocks of 16 rows) name no expert more than 2 times, and there is at least one expert (the same one in every block) that every such block names exactly 2 times.
All inputs are finite; a program needn't handle non-finite values.
Results may differ from the reference program's by a relative error of at most 0.0065.
Values may be sent and summed in bfloat16 or wider, within the bound.
No kernel may reach another device: no remote copies, remote signals or barrier semaphores. Data moves between devices by JAX's collectives and lax.ppermute only.
A program may use at most 64 MiB of HBM per device.

```python
import math
import jax
import jax.numpy as jnp
from jax import lax

ROWS_DEV = 16
D = 3584
FF = 1024
FFH = 512
TOPK = 8
GROUPS = 8
EXPERTS = 128
EXP_GROUP = 16
MOST = 2
TOKENS = 4096


def draw_expert_ids(key, part):
    key = jax.random.fold_in(key, 7)
    key_hot, key_pick, key_perm, key_order = jax.random.split(key, 4)
    blocks = TOKENS // ROWS_DEV
    hot_group = jax.random.randint(key_hot, (), 0, GROUPS)
    group_ids = jnp.arange(GROUPS, dtype=jnp.int32)
    scores = jax.random.randint(key_pick, (TOKENS, GROUPS), 0, 1 << 20) * GROUPS + group_ids[None, :]
    scores = jnp.where(group_ids[None, :] == hot_group, 1 << 28, scores)
    chosen = lax.top_k(scores, 4)[1].astype(jnp.int32)
    member = jnp.sum((chosen[:, :, None] == group_ids[None, None, :]).astype(jnp.int32), axis=1)
    member = member.reshape(blocks, ROWS_DEV, GROUPS)
    row_ranks = (jnp.cumsum(member, axis=1) - member).reshape(TOKENS, GROUPS)
    perm_scores = jax.random.randint(key_perm, (blocks, GROUPS, EXP_GROUP), 0, 1 << 20) * EXP_GROUP
    perm_scores = perm_scores + jnp.arange(EXP_GROUP, dtype=jnp.int32)
    expert_perms = jnp.argsort(perm_scores, axis=-1).astype(jnp.int32)
    row_block = jnp.arange(TOKENS, dtype=jnp.int32) // ROWS_DEV
    rank_chosen = jnp.take_along_axis(row_ranks, chosen, axis=1)
    slot_first = 2 * rank_chosen % EXP_GROUP
    slot_second = (2 * rank_chosen + 1) % EXP_GROUP
    group_table = expert_perms[row_block[:, None], chosen]
    pick_one = jnp.take_along_axis(group_table, slot_first[:, :, None], axis=2)[:, :, 0]
    pick_two = jnp.take_along_axis(group_table, slot_second[:, :, None], axis=2)[:, :, 0]
    experts = jnp.stack([chosen * EXP_GROUP + pick_one, chosen * EXP_GROUP + pick_two], axis=2)
    experts = experts.reshape(TOKENS, TOPK)
    order_scores = jax.random.randint(key_order, (TOKENS, TOPK), 0, 1 << 20) * TOPK
    order_scores = order_scores + jnp.arange(TOPK, dtype=jnp.int32)
    shuffle = jnp.argsort(order_scores, axis=1)
    return jnp.take_along_axis(experts, shuffle, axis=1).astype(jnp.int32)


def level_of(own_key, dims, cuts, smallest, largest):
    def one(dim, blocks):
        draws = jax.random.uniform(jax.random.fold_in(jax.random.fold_in(own_key, 6), dim), (blocks,), jnp.float32, smallest / len(cuts), largest / len(cuts))
        return jnp.repeat(jnp.exp(draws), dims[dim] // blocks).reshape((-1,) + (1,) * (len(dims) - dim - 1))

    loudness = one(*cuts[0])
    for cut in cuts[1:]:
        loudness = loudness * one(*cut)
    return loudness


def bell_draw(stream_key, extent, spread, reach, pieces=(), held_as=jnp.bfloat16):
    result = spread * jax.random.normal(stream_key, extent, jnp.float32)
    if pieces:
        result = result * level_of(stream_key, extent, pieces, -0.22, 0.18)
    return jnp.clip(result, -reach, reach).astype(held_as)


def setup_inputs(seed: int = 0) -> dict:
    splits = jax.random.split(jax.random.key(seed), 7)
    tokens = bell_draw(splits[0], (TOKENS, D), 1.0, 6.0, ((0, 256),))
    expert_ids = draw_expert_ids(jax.random.fold_in(splits[6], 71), 0)
    gates = jnp.clip(jnp.exp(math.log(0.6) - 1.7917595 * jax.random.uniform(splits[2], (TOKENS, TOPK), jnp.float32) ** level_of(splits[2], (TOKENS, TOPK), ((0, 256),), -0.2, 0.2)), 0.1, 0.6)
    gate_weight = bell_draw(splits[3], (2 * EXPERTS, D, FFH), D ** -0.5, 0.09375, ((0, 256),))
    up_weight = bell_draw(splits[4], (2 * EXPERTS, D, FFH), D ** -0.5, 0.09375, ((0, 256),))
    down_weight = bell_draw(splits[5], (2 * EXPERTS, FFH, D), FF ** -0.5, 0.1875, ((0, 256),))
    return dict(tokens=tokens, expert_ids=expert_ids, gates=gates, gate_weight=gate_weight, up_weight=up_weight, down_weight=down_weight)


def reference(tokens, expert_ids, gates, gate_weight, up_weight, down_weight):
    capacity = (TOKENS // ROWS_DEV) * MOST
    pair_expert = expert_ids.reshape(-1)
    pair_row = (jnp.arange(TOKENS * TOPK, dtype=jnp.int32) // TOPK).astype(jnp.int32)
    pair_gate = gates.reshape(-1)

    def one_expert(mixed_sum, expert):
        match_mask = pair_expert == expert
        pair_index = jnp.nonzero(match_mask, size=capacity, fill_value=0)[0].astype(jnp.int32)
        live_count = jnp.sum(match_mask.astype(jnp.int32))
        live_mask = jnp.arange(capacity, dtype=jnp.int32) < live_count
        row_index = pair_row[pair_index]
        row_data = tokens[row_index]
        halves = []
        for half_index in range(2):
            slab = (2 * expert + half_index).astype(jnp.int32)
            gate_half = lax.dynamic_index_in_dim(gate_weight, slab, 0, keepdims=False)
            up_half = lax.dynamic_index_in_dim(up_weight, slab, 0, keepdims=False)
            down_half = lax.dynamic_index_in_dim(down_weight, slab, 0, keepdims=False)
            gate_proj = jnp.dot(row_data, gate_half, preferred_element_type=jnp.float32)
            up_proj = jnp.dot(row_data, up_half, preferred_element_type=jnp.float32)
            hidden = (jax.nn.silu(gate_proj) * up_proj).astype(jnp.bfloat16)
            half_out = jnp.dot(hidden, down_half, preferred_element_type=jnp.float32).astype(jnp.bfloat16)
            halves.append(lax.optimization_barrier(half_out).astype(jnp.float32))
        expert_out = (halves[0] + halves[1]).astype(jnp.bfloat16)
        expert_out = lax.optimization_barrier(expert_out).astype(jnp.float32)
        weight_live = jnp.where(live_mask, pair_gate[pair_index], jnp.zeros((), jnp.float32))
        mixed_sum = mixed_sum.at[row_index].add(weight_live[:, None] * expert_out)
        return mixed_sum, None

    start_sum = jnp.zeros((TOKENS, D), jnp.float32)
    mixed_sum, _ = lax.scan(one_expert, start_sum, jnp.arange(EXPERTS, dtype=jnp.int32))
    return mixed_sum.astype(jnp.bfloat16)
```

```python
import jax
import jax.numpy as jnp
from jax import lax
from jax.experimental import pallas as pl
from jax.experimental.pallas import tpu as pltpu
from jax.sharding import Mesh, PartitionSpec as P

Z, Y, X, C = 8, 4, 4, 2
PLANE = Y * X
SLOTS = 2
TAIL = 128
BF = jnp.bfloat16
F32 = jnp.float32
MIB = 1 << 20


def along(shift):
    pairs = []
    for z in range(Z):
        pairs.append((z * C, (z + shift) % Z * C))
        pairs.append((z * C + 1, (z - shift) % Z * C + 1))
    return pairs


def send(value, shift):
    return lax.ppermute(value, ("z", "c"), along(shift))


def swap(value):
    return lax.ppermute(value, "c", [(0, 1), (1, 0)])


def place_kernel(own, near, second, third, fourth, rows_out, high_out, low_out):
    pieces = (own, near, second, third, fourth)
    width = rows_out.shape[1]
    rows = sum(p.shape[0] for p in pieces)
    block = own.shape[0]
    blocks = rows // block
    per_expert = blocks * SLOTS
    slots = PLANE * per_expert
    tail = jnp.concatenate([p[:, width:] for p in pieces], axis=0).astype(F32).T
    expert = (lax.axis_index("z") * PLANE + lax.broadcasted_iota(jnp.int32, (PLANE, rows), 0)).astype(F32)
    named = jnp.zeros((PLANE, rows), F32)
    gate = jnp.zeros((PLANE, rows), F32)
    for k in range(8):
        hit = tail[k : k + 1] == expert
        value = tail[8 + k : 9 + k] + tail[16 + k : 17 + k] + tail[24 + k : 25 + k]
        named = named + jnp.where(hit, 1.0, 0.0)
        gate = gate + jnp.where(hit, value, 0.0)
    before = lax.broadcasted_iota(jnp.int32, (rows, rows), 0)
    after = lax.broadcasted_iota(jnp.int32, (rows, rows), 1)
    earlier = jnp.where((before < after) & (before // block == after // block), 1.0, 0.0).astype(BF)
    rank = jnp.dot(named.astype(BF), earlier, preferred_element_type=F32)

    def spread(value):
        return jnp.broadcast_to(value[:, None, :], (PLANE, per_expert, rows)).reshape(slots, rows)

    slot = lax.broadcasted_iota(jnp.int32, (slots, rows), 0)
    lane = lax.broadcasted_iota(jnp.int32, (slots, rows), 1)
    here = (slot // SLOTS) % blocks == lane // block
    chosen = here & (spread(named) > 0.5) & (spread(rank) == (slot % SLOTS).astype(F32))
    weight = jnp.where(chosen, spread(gate), 0.0)
    high = weight.astype(BF)
    high_out[...] = high
    low_out[...] = (weight - high.astype(F32)).astype(BF)
    pick = jnp.where(chosen, 1.0, 0.0).astype(BF)
    step = 512
    for c in range(0, width, step):
        part = jnp.concatenate([p[:, c : c + step] for p in pieces], axis=0)
        rows_out[:, c : c + step] = jnp.dot(pick, part, preferred_element_type=F32).astype(BF)


def place(pieces, width):
    rows = sum(p.shape[0] for p in pieces)
    slots = PLANE * SLOTS * (rows // pieces[0].shape[0])
    return pl.pallas_call(
        place_kernel,
        out_shape=(
            jax.ShapeDtypeStruct((slots, width), BF),
            jax.ShapeDtypeStruct((slots, rows), BF),
            jax.ShapeDtypeStruct((slots, rows), BF),
        ),
        compiler_params=pltpu.CompilerParams(vmem_limit_bytes=24 * MIB),
        name="place",
    )(*pieces)


def expert_kernel(rows, gate_a, up_a, down_a, gate_b, up_b, down_b, out, gate_v, up_v, down_v, hidden, sems):
    width, half = gate_a.shape
    tile = 256
    tiles = half // tile
    cut = width // 2
    ins = []
    for h, (g, u) in enumerate(((gate_a, up_a), (gate_b, up_b))):
        for j in range(tiles):
            where = pl.ds(j * tile, tile)
            for m, (src, dst) in enumerate(((g, gate_v), (u, up_v))):
                ins.append(pltpu.make_async_copy(src.at[:, where], dst.at[h, :, where], sems.at[(h * tiles + j) * 2 + m]))
    downs = []
    for j in range(2):
        for h, d in enumerate((down_a, down_b)):
            where = pl.ds(j * cut, cut)
            downs.append(pltpu.make_async_copy(d.at[:, where], down_v.at[pl.ds(h * half, half), where], sems.at[4 * tiles + j * 2 + h]))
    for copy in ins + downs:
        copy.start()
    for i in range(2 * tiles):
        h, j = i // tiles, i % tiles
        ins[2 * i].wait()
        ins[2 * i + 1].wait()
        g = jnp.dot(rows[...], gate_v[h, :, j * tile : (j + 1) * tile], preferred_element_type=F32)
        u = jnp.dot(rows[...], up_v[h, :, j * tile : (j + 1) * tile], preferred_element_type=F32)
        hidden[:, i * tile : (i + 1) * tile] = (g / (1.0 + jnp.exp(-g)) * u).astype(BF)
    step = 256
    for j in range(2):
        downs[2 * j].wait()
        downs[2 * j + 1].wait()
        for c in range(j * cut, (j + 1) * cut, step):
            out[:, c : c + step] = jnp.dot(hidden[...], down_v[:, c : c + step], preferred_element_type=F32).astype(BF)


def experts(rows, own, other):
    width, half = own[0].shape
    count = rows.shape[0]
    vmem = pl.BlockSpec(memory_space=pltpu.VMEM)
    anywhere = pl.BlockSpec(memory_space=pl.ANY)
    return pl.pallas_call(
        expert_kernel,
        out_shape=jax.ShapeDtypeStruct((count, width), BF),
        in_specs=[vmem] + [anywhere] * 6,
        out_specs=vmem,
        scratch_shapes=[
            pltpu.VMEM((2, width, half), BF),
            pltpu.VMEM((2, width, half), BF),
            pltpu.VMEM((2 * half, width), BF),
            pltpu.VMEM((count, 2 * half), BF),
            pltpu.SemaphoreType.DMA((4 * (half // 256) + 4,)),
        ],
        compiler_params=pltpu.CompilerParams(vmem_limit_bytes=40 * MIB),
        cost_estimate=pl.CostEstimate(
            flops=2 * count * width * half * 6, bytes_accessed=12 * width * half + 4 * count * width, transcendentals=2 * count * half
        ),
        name="experts",
    )(rows, *own, *other)


def collect_kernel(returned, high, low, own_out, near_out, second_out, third_out, fourth_out):
    width = returned.shape[1]
    step = 512
    across = (((0,), (0,)), ((), ()))
    for c in range(0, width, step):
        part = returned[:, c : c + step]
        total = lax.dot_general(high[...], part, across, preferred_element_type=F32)
        total = total + lax.dot_general(low[...], part, across, preferred_element_type=F32)
        start = 0
        for ref in (own_out, near_out, second_out, third_out, fourth_out):
            count = ref.shape[0]
            ref[:, c : c + step] = total[start : start + count].astype(ref.dtype)
            start += count


def collect(returned, high, low, block):
    width = returned.shape[1]

    def shape(blocks, kind):
        return jax.ShapeDtypeStruct((blocks * block, width), kind)

    return pl.pallas_call(
        collect_kernel,
        out_shape=(shape(1, F32), shape(2, BF), shape(2, F32), shape(2, BF), shape(1, BF)),
        compiler_params=pltpu.CompilerParams(vmem_limit_bytes=24 * MIB),
        name="collect",
    )(returned, high, low)


def body(tokens, expert_ids, gates, gate_weight, up_weight, down_weight):
    block, width = tokens.shape
    own_weights = (gate_weight[0], up_weight[0], down_weight[0])
    other_weights = tuple(swap(w) for w in own_weights)
    high = lax.reduce_precision(gates, 8, 7)
    rest = gates - high
    middle = lax.reduce_precision(rest, 8, 7)
    low = rest - middle
    used = 4 * expert_ids.shape[1]
    tail = [v.astype(BF) for v in (expert_ids, high, middle, low)] + [jnp.zeros((block, TAIL - used), BF)]
    own = jnp.concatenate([tokens] + tail, axis=1)
    both = jnp.concatenate([own, swap(own)], axis=0)
    second = send(both, 2)
    near = send(both, 1)
    third = send(second, 1)
    fourth = send(second[:block], 2)
    placed, weight_high, weight_low = place((own, near, second, third, fourth), width)
    arrived = lax.all_to_all(placed.reshape(PLANE, -1, width), ("y", "x"), 0, 0, tiled=True)
    done = experts(arrived.reshape(-1, width), own_weights, other_weights)
    returned = lax.all_to_all(done.reshape(PLANE, -1, width), ("y", "x"), 0, 0, tiled=True)
    q_own, q_near, q_second, q_third, q_fourth = collect(returned.reshape(-1, width), weight_high, weight_low, block)
    from_third = send(q_third, -1)
    from_fourth = send(q_fourth, -2)
    from_near = send(q_near, -1)
    first_half = q_second[:block] + from_third[:block].astype(F32) + from_fourth.astype(F32)
    second_half = q_second[block:] + from_third[block:].astype(F32)
    from_second = send(jnp.concatenate([first_half, second_half], axis=0).astype(BF), -2)
    total = from_near.astype(F32) + from_second.astype(F32)
    from_core = swap(total[block:].astype(BF))
    return (q_own + total[:block] + from_core.astype(F32)).astype(BF)


def solution(mesh):
    fine = Mesh(mesh.devices.reshape(Z, Y, X, C), ("z", "y", "x", "c"))
    rows = P(("z", "y", "x", "c"))
    return jax.shard_map(body, mesh=fine, in_specs=(rows,) * 6, out_specs=rows, check_vma=False)
```

```python
import jax
import jax.numpy as jnp
from jax import lax
from jax.experimental import pallas as pl
from jax.experimental.pallas import tpu as pltpu
from jax.sharding import Mesh, PartitionSpec as P

Z, Y, X, C = 8, 4, 4, 2
PLANE = Y * X
SLOTS = 2
TAIL = 128
BF = jnp.bfloat16
F32 = jnp.float32
MIB = 1 << 20
VMEM = pl.BlockSpec(memory_space=pltpu.VMEM)


def along(shift):
    pairs = []
    for z in range(Z):
        pairs.append((z * C, (z + shift) % Z * C))
        pairs.append((z * C + 1, (z - shift) % Z * C + 1))
    return pairs


def across(shift):
    pairs = []
    for z in range(Z):
        pairs.append((z * C, (z - shift) % Z * C + 1))
        pairs.append((z * C + 1, (z + shift) % Z * C))
    return pairs


def send(value, shift):
    return lax.ppermute(value, ("z", "c"), along(shift))


def back_across(value, shift):
    return lax.ppermute(value, ("z", "c"), across(shift))


def swap(value):
    return lax.ppermute(value, "c", [(0, 1), (1, 0)])


def extend_kernel(tokens, ids, gates, out):
    block, width = tokens.shape
    gate = gates[...]
    high = gate.astype(BF)
    rest = gate - high.astype(F32)
    middle = rest.astype(BF)
    low = (rest - middle.astype(F32)).astype(BF)
    parts = [v.astype(F32) for v in (ids[...], high, middle, low)]
    used = sum(p.shape[0] for p in parts)
    parts.append(jnp.zeros((TAIL - used, block), F32))
    table = jnp.concatenate(parts, axis=0).astype(BF)
    left = lax.broadcasted_iota(jnp.int32, (block, block), 0)
    right = lax.broadcasted_iota(jnp.int32, (block, block), 1)
    unit = jnp.where(left == right, 1.0, 0.0).astype(BF)
    tail = lax.dot_general(unit, table, (((1,), (1,)), ((), ())), preferred_element_type=F32)
    out[:, :width] = tokens[...]
    out[:, width:] = tail.astype(BF)


def extend(tokens, expert_ids, gates):
    block, width = tokens.shape
    return pl.pallas_call(
        extend_kernel,
        out_shape=jax.ShapeDtypeStruct((block, width + TAIL), BF),
        name="extend",
    )(tokens, expert_ids.T, gates.T)


def place_kernel(block, *refs):
    pieces, (rows_out, high_out, low_out) = list(refs[:-3]), refs[-3:]
    pieces[0] = pieces[0].at[:block]
    width = rows_out.shape[1]
    rows = sum(p.shape[0] for p in pieces)
    blocks = rows // block
    per_expert = blocks * SLOTS
    slots = PLANE * per_expert
    tail = [p[:, width:].astype(F32) for p in pieces]
    if rows < TAIL:
        tail.append(jnp.zeros((TAIL - rows, TAIL), F32))
    tail = jnp.concatenate(tail, axis=0).T[:, :rows]
    expert = (lax.axis_index("z") * PLANE + lax.broadcasted_iota(jnp.int32, (PLANE, rows), 0)).astype(F32)
    named = jnp.zeros((PLANE, rows), F32)
    gate = jnp.zeros((PLANE, rows), F32)
    for k in range(8):
        hit = tail[k : k + 1] == expert
        value = tail[8 + k : 9 + k] + tail[16 + k : 17 + k] + tail[24 + k : 25 + k]
        named = named + jnp.where(hit, 1.0, 0.0)
        gate = gate + jnp.where(hit, value, 0.0)
    before = lax.broadcasted_iota(jnp.int32, (rows, rows), 0)
    after = lax.broadcasted_iota(jnp.int32, (rows, rows), 1)
    earlier = jnp.where((before < after) & (before // block == after // block), 1.0, 0.0).astype(BF)
    rank = jnp.dot(named.astype(BF), earlier, preferred_element_type=F32)

    def spread(value):
        return jnp.broadcast_to(value[:, None, :], (PLANE, per_expert, rows)).reshape(slots, rows)

    slot = lax.broadcasted_iota(jnp.int32, (slots, rows), 0)
    lane = lax.broadcasted_iota(jnp.int32, (slots, rows), 1)
    here = (slot // SLOTS) % blocks == lane // block
    chosen = here & (spread(named) > 0.5) & (spread(rank) == (slot % SLOTS).astype(F32))
    weight = jnp.where(chosen, spread(gate), 0.0)
    high = weight.astype(BF)
    high_out[...] = high
    low_out[...] = (weight - high.astype(F32)).astype(BF)
    pick = jnp.where(chosen, 1.0, 0.0).astype(BF)
    step = 512
    for c in range(0, width, step):
        part = jnp.concatenate([p[:, c : c + step] for p in pieces], axis=0)
        rows_out[:, c : c + step] = jnp.dot(pick, part, preferred_element_type=F32).astype(BF)


def place(pieces, block, width):
    rows = sum(p.shape[0] for p in pieces) - block
    slots = PLANE * SLOTS * (rows // block)

    def kernel(*refs):
        place_kernel(block, *refs)

    return pl.pallas_call(
        kernel,
        out_shape=(
            jax.ShapeDtypeStruct((slots, width), BF),
            jax.ShapeDtypeStruct((slots, rows), BF),
            jax.ShapeDtypeStruct((slots, rows), BF),
        ),
        compiler_params=pltpu.CompilerParams(vmem_limit_bytes=16 * MIB),
        cost_estimate=pl.CostEstimate(flops=2 * slots * rows * width, bytes_accessed=2 * (slots + rows) * width, transcendentals=0),
        name="place",
    )(*pieces)


def expert_kernel(rows, gate_a, up_a, down_a, gate_b, up_b, down_b, out, gate_v, up_v, down_v, hidden, sems):
    half = gate_a.shape[1]
    width = out.shape[1]
    pairs = ((gate_a, gate_v), (up_a, up_v), (down_a, down_v))
    copies = [pltpu.make_async_copy(src, dst, sems.at[i]) for i, (src, dst) in enumerate(pairs)]
    for copy in copies:
        copy.start()
    tile = 256
    for h, (gate, up) in enumerate(((gate_b, up_b), (gate_v, up_v))):
        if h == 1:
            copies[0].wait()
            copies[1].wait()
        for j in range(0, half, tile):
            g = jnp.dot(rows[...], gate[:, j : j + tile], preferred_element_type=F32)
            u = jnp.dot(rows[...], up[:, j : j + tile], preferred_element_type=F32)
            hidden[:, h * half + j : h * half + j + tile] = (g / (1.0 + jnp.exp(-g)) * u).astype(BF)
    copies[2].wait()
    for c in range(0, width, tile):
        total = jnp.dot(hidden[:, :half], down_b[:, c : c + tile], preferred_element_type=F32)
        total = total + jnp.dot(hidden[:, half:], down_v[:, c : c + tile], preferred_element_type=F32)
        out[:, c : c + tile] = total.astype(BF)


def experts(rows, own, other):
    width, half = own[0].shape
    count = rows.shape[0]
    return pl.pallas_call(
        expert_kernel,
        out_shape=jax.ShapeDtypeStruct(rows.shape, BF),
        in_specs=[VMEM] + [pl.BlockSpec(memory_space=pl.ANY)] * 3 + [VMEM] * 3,
        out_specs=VMEM,
        scratch_shapes=[
            pltpu.VMEM((width, half), BF),
            pltpu.VMEM((width, half), BF),
            pltpu.VMEM((half, width), BF),
            pltpu.VMEM((count, 2 * half), BF),
            pltpu.SemaphoreType.DMA((3,)),
        ],
        compiler_params=pltpu.CompilerParams(vmem_limit_bytes=32 * MIB),
        cost_estimate=pl.CostEstimate(
            flops=2 * count * width * half * 6, bytes_accessed=12 * width * half + 4 * count * width, transcendentals=2 * count * half
        ),
        name="experts",
    )(rows, *own, *other)


def collect_kernel(returned, high, low, *outs):
    step = 512
    over = (((0,), (0,)), ((), ()))
    for c in range(0, returned.shape[1], step):
        part = returned[:, c : c + step]
        total = lax.dot_general(high[...], part, over, preferred_element_type=F32)
        total = total + lax.dot_general(low[...], part, over, preferred_element_type=F32)
        start = 0
        for out in outs:
            count = out.shape[0]
            out[:, c : c + step] = total[start : start + count].astype(out.dtype)
            start += count


def collect(returned, high, low, shapes):
    slots, width = returned.shape
    rows = high.shape[1]
    return pl.pallas_call(
        collect_kernel,
        out_shape=[jax.ShapeDtypeStruct((count, width), kind) for count, kind in shapes],
        compiler_params=pltpu.CompilerParams(vmem_limit_bytes=16 * MIB),
        cost_estimate=pl.CostEstimate(flops=4 * slots * rows * width, bytes_accessed=2 * (slots + rows) * width, transcendentals=0),
        name="collect",
    )(returned, high, low)


def exchange(value):
    width = value.shape[1]
    return lax.all_to_all(value.reshape(PLANE, -1, width), ("y", "x"), 0, 0, tiled=True).reshape(-1, width)


def body(tokens, expert_ids, gates, gate_weight, up_weight, down_weight):
    block, width = tokens.shape
    own_weights = [gate_weight[0], up_weight[0], down_weight[0]]
    own = extend(tokens, expert_ids, gates)
    other, sent_weights = lax.optimization_barrier((swap(own), own_weights))
    other_weights = [swap(w) for w in sent_weights]
    own_weights = [pltpu.with_memory_space_constraint(w, pltpu.HBM) for w in own_weights]
    other_weights = [pltpu.with_memory_space_constraint(w, pltpu.VMEM) for w in other_weights]

    both = jnp.concatenate([own, other], axis=0)
    second = send(both, 2)
    near = send(both, 1)
    third = send(second, 1)
    fourth = send(second[:block], 2)
    rows, high, low = place((both, near, second, third, fourth), block, width)
    done = experts(exchange(rows), own_weights, other_weights)
    returned = exchange(done)
    shapes = ((block, F32), (block, BF), (block, BF), (block, F32), (block, F32), (2 * block, BF), (block, BF))
    q_own, q_near, q_near_other, q_second, q_second_other, q_third, q_fourth = collect(returned, high, low, shapes)
    third = send(q_third, -1)
    fourth = send(q_fourth, -2)
    near = send(q_near, -1)
    near_other = back_across(q_near_other, 1)
    second = send((q_second + third[:block].astype(F32) + fourth.astype(F32)).astype(BF), -2)
    second_other = back_across((q_second_other + third[block:].astype(F32)).astype(BF), 2)
    total = q_own + near.astype(F32) + near_other.astype(F32)
    return (total + second.astype(F32) + second_other.astype(F32)).astype(BF)


def solution(mesh):
    fine = Mesh(mesh.devices.reshape(Z, Y, X, C), ("z", "y", "x", "c"))
    rows = P(("z", "y", "x", "c"))
    return jax.shard_map(body, mesh=fine, in_specs=(rows,) * 6, out_specs=rows, check_vma=False)
```

```python
import jax
import jax.numpy as jnp
from jax import lax
from jax.experimental import pallas as pl
from jax.experimental.pallas import tpu as pltpu
from jax.sharding import Mesh, PartitionSpec as P

Z, PAIR, Y, X, C = 4, 2, 4, 4, 2
PLANE = PAIR * Y * X
SLOTS = 2
TAIL = 128
BF = jnp.bfloat16
F32 = jnp.float32
MIB = 1 << 20
VMEM = pl.BlockSpec(memory_space=pltpu.VMEM)


def along(shift):
    pairs = []
    for z in range(Z):
        pairs.append((z * C, (z + shift) % Z * C))
        pairs.append((z * C + 1, (z - shift) % Z * C + 1))
    return pairs


def across(shift):
    pairs = []
    for z in range(Z):
        pairs.append((z * C, (z - shift) % Z * C + 1))
        pairs.append((z * C + 1, (z + shift) % Z * C))
    return pairs


def send(value, shift):
    return lax.ppermute(value, ("s", "c"), along(shift))


def back_across(value, shift):
    return lax.ppermute(value, ("s", "c"), across(shift))


def swap(value):
    return lax.ppermute(value, "c", [(0, 1), (1, 0)])


def extend_kernel(tokens, ids, gates, out):
    block, width = tokens.shape
    gate = gates[...]
    high = gate.astype(BF)
    rest = gate - high.astype(F32)
    middle = rest.astype(BF)
    low = (rest - middle.astype(F32)).astype(BF)
    parts = [v.astype(F32) for v in (ids[...], high, middle, low)]
    used = sum(p.shape[0] for p in parts)
    parts.append(jnp.zeros((TAIL - used, block), F32))
    table = jnp.concatenate(parts, axis=0).astype(BF)
    left = lax.broadcasted_iota(jnp.int32, (block, block), 0)
    right = lax.broadcasted_iota(jnp.int32, (block, block), 1)
    unit = jnp.where(left == right, 1.0, 0.0).astype(BF)
    tail = lax.dot_general(unit, table, (((1,), (1,)), ((), ())), preferred_element_type=F32)
    out[:, :width] = tokens[...]
    out[:, width:] = tail.astype(BF)


def extend(tokens, expert_ids, gates):
    block, width = tokens.shape
    return pl.pallas_call(
        extend_kernel,
        out_shape=jax.ShapeDtypeStruct((block, width + TAIL), BF),
        name="extend",
    )(tokens, expert_ids.T, gates.T)


def place_kernel(block, *refs):
    pieces, (rows_out, high_out, low_out) = list(refs[:-3]), refs[-3:]
    pieces[0] = pieces[0].at[:block]
    width = rows_out.shape[1]
    rows = sum(p.shape[0] for p in pieces)
    blocks = rows // block
    per_expert = blocks * SLOTS
    slots = PLANE * per_expert
    tail = [p[:, width:].astype(F32) for p in pieces]
    if rows < TAIL:
        tail.append(jnp.zeros((TAIL - rows, TAIL), F32))
    tail = jnp.concatenate(tail, axis=0).T[:, :rows]
    expert = (lax.axis_index("s") * PLANE + lax.broadcasted_iota(jnp.int32, (PLANE, rows), 0)).astype(F32)
    named = jnp.zeros((PLANE, rows), F32)
    gate = jnp.zeros((PLANE, rows), F32)
    for k in range(8):
        hit = tail[k : k + 1] == expert
        value = tail[8 + k : 9 + k] + tail[16 + k : 17 + k] + tail[24 + k : 25 + k]
        named = named + jnp.where(hit, 1.0, 0.0)
        gate = gate + jnp.where(hit, value, 0.0)
    before = lax.broadcasted_iota(jnp.int32, (rows, rows), 0)
    after = lax.broadcasted_iota(jnp.int32, (rows, rows), 1)
    earlier = jnp.where((before < after) & (before // block == after // block), 1.0, 0.0).astype(BF)
    rank = jnp.dot(named.astype(BF), earlier, preferred_element_type=F32)

    def spread(value):
        return jnp.broadcast_to(value[:, None, :], (PLANE, per_expert, rows)).reshape(slots, rows)

    slot = lax.broadcasted_iota(jnp.int32, (slots, rows), 0)
    lane = lax.broadcasted_iota(jnp.int32, (slots, rows), 1)
    here = (slot // SLOTS) % blocks == lane // block
    chosen = here & (spread(named) > 0.5) & (spread(rank) == (slot % SLOTS).astype(F32))
    weight = jnp.where(chosen, spread(gate), 0.0)
    high = weight.astype(BF)
    high_out[...] = high
    low_out[...] = (weight - high.astype(F32)).astype(BF)
    pick = jnp.where(chosen, 1.0, 0.0).astype(BF)
    step = 512
    for c in range(0, width, step):
        part = jnp.concatenate([p[:, c : c + step] for p in pieces], axis=0)
        rows_out[:, c : c + step] = jnp.dot(pick, part, preferred_element_type=F32).astype(BF)


def place(pieces, block, width):
    rows = sum(p.shape[0] for p in pieces) - block
    slots = PLANE * SLOTS * (rows // block)

    def kernel(*refs):
        place_kernel(block, *refs)

    return pl.pallas_call(
        kernel,
        out_shape=(
            jax.ShapeDtypeStruct((slots, width), BF),
            jax.ShapeDtypeStruct((slots, rows), BF),
            jax.ShapeDtypeStruct((slots, rows), BF),
        ),
        compiler_params=pltpu.CompilerParams(vmem_limit_bytes=16 * MIB),
        cost_estimate=pl.CostEstimate(flops=2 * slots * rows * width, bytes_accessed=2 * (slots + rows) * width, transcendentals=0),
        name="place",
    )(*pieces)


def expert_kernel(rows, gate_a, up_a, down_a, gate_b, up_b, down_b, out, gate_v, up_v, down_v, hidden, sems):
    half = gate_a.shape[1]
    width = out.shape[1]
    pairs = ((gate_a, gate_v), (up_a, up_v), (down_a, down_v))
    copies = [pltpu.make_async_copy(src, dst, sems.at[i]) for i, (src, dst) in enumerate(pairs)]
    for copy in copies:
        copy.start()
    tile = 256
    for h, (gate, up) in enumerate(((gate_b, up_b), (gate_v, up_v))):
        if h == 1:
            copies[0].wait()
            copies[1].wait()
        for j in range(0, half, tile):
            g = jnp.dot(rows[...], gate[:, j : j + tile], preferred_element_type=F32)
            u = jnp.dot(rows[...], up[:, j : j + tile], preferred_element_type=F32)
            hidden[:, h * half + j : h * half + j + tile] = (g / (1.0 + jnp.exp(-g)) * u).astype(BF)
    copies[2].wait()
    for c in range(0, width, tile):
        total = jnp.dot(hidden[:, :half], down_b[:, c : c + tile], preferred_element_type=F32)
        total = total + jnp.dot(hidden[:, half:], down_v[:, c : c + tile], preferred_element_type=F32)
        out[:, c : c + tile] = total.astype(BF)


def experts(rows, own, other):
    width, half = own[0].shape
    count = rows.shape[0]
    return pl.pallas_call(
        expert_kernel,
        out_shape=jax.ShapeDtypeStruct(rows.shape, BF),
        in_specs=[VMEM] + [pl.BlockSpec(memory_space=pl.ANY)] * 3 + [VMEM] * 3,
        out_specs=VMEM,
        scratch_shapes=[
            pltpu.VMEM((width, half), BF),
            pltpu.VMEM((width, half), BF),
            pltpu.VMEM((half, width), BF),
            pltpu.VMEM((count, 2 * half), BF),
            pltpu.SemaphoreType.DMA((3,)),
        ],
        compiler_params=pltpu.CompilerParams(vmem_limit_bytes=32 * MIB),
        cost_estimate=pl.CostEstimate(
            flops=2 * count * width * half * 6, bytes_accessed=12 * width * half + 4 * count * width, transcendentals=2 * count * half
        ),
        name="experts",
    )(rows, *own, *other)


def collect_kernel(returned, high, low, *outs):
    step = 512
    over = (((0,), (0,)), ((), ()))
    for c in range(0, returned.shape[1], step):
        part = returned[:, c : c + step]
        total = lax.dot_general(high[...], part, over, preferred_element_type=F32)
        total = total + lax.dot_general(low[...], part, over, preferred_element_type=F32)
        start = 0
        for out in outs:
            count = out.shape[0]
            out[:, c : c + step] = total[start : start + count].astype(out.dtype)
            start += count


def collect(returned, high, low, shapes):
    slots, width = returned.shape
    rows = high.shape[1]
    return pl.pallas_call(
        collect_kernel,
        out_shape=[jax.ShapeDtypeStruct((count, width), kind) for count, kind in shapes],
        compiler_params=pltpu.CompilerParams(vmem_limit_bytes=16 * MIB),
        cost_estimate=pl.CostEstimate(flops=4 * slots * rows * width, bytes_accessed=2 * (slots + rows) * width, transcendentals=0),
        name="collect",
    )(returned, high, low)


def exchange(value):
    width = value.shape[1]
    return lax.all_to_all(value.reshape(PLANE, -1, width), ("p", "y", "x"), 0, 0, tiled=True).reshape(-1, width)


def body(tokens, expert_ids, gates, gate_weight, up_weight, down_weight):
    block, width = tokens.shape
    own_weights = [gate_weight[0], up_weight[0], down_weight[0]]
    own = extend(tokens, expert_ids, gates)
    other, sent_weights = lax.optimization_barrier((swap(own), own_weights))
    other_weights = [swap(w) for w in sent_weights]
    own_weights = [pltpu.with_memory_space_constraint(w, pltpu.HBM) for w in own_weights]

    both = jnp.concatenate([own, other], axis=0)
    far = send(own, 2)
    near = send(both, 1)
    rows, high, low = place((both, near, far), block, width)
    rows, other_weights = lax.optimization_barrier((rows, other_weights))
    other_weights = [pltpu.with_memory_space_constraint(w, pltpu.VMEM) for w in other_weights]
    done = experts(exchange(rows), own_weights, other_weights)
    returned = exchange(done)
    shapes = ((block, F32), (block, BF), (block, BF), (block, BF))
    q_own, q_near, q_near_other, q_far = collect(returned, high, low, shapes)
    far = send(q_far, -2)
    near = send(q_near, -1)
    near_other = back_across(q_near_other, 1)
    return (q_own + near.astype(F32) + near_other.astype(F32) + far.astype(F32)).astype(BF)


def solution(mesh):
    names = ("s", "p", "y", "x", "c")
    fine = Mesh(mesh.devices.reshape(Z, PAIR, Y, X, C), names)
    rows = P(names)
    return jax.shard_map(body, mesh=fine, in_specs=(rows,) * 6, out_specs=rows, check_vma=False)
```

```python
import jax
import jax.numpy as jnp
from jax import lax
from jax.experimental import pallas as pl
from jax.experimental.pallas import tpu as pltpu
from jax.sharding import Mesh, PartitionSpec as P

Z, PAIR, Y, X, C = 4, 2, 4, 4, 2
PLANE = PAIR * Y * X
SLOTS = 2
TAIL = 128
BF = jnp.bfloat16
F32 = jnp.float32
MIB = 1 << 20
VMEM = pl.BlockSpec(memory_space=pltpu.VMEM)


def along(shift):
    pairs = []
    for z in range(Z):
        pairs.append((z * C, (z + shift) % Z * C))
        pairs.append((z * C + 1, (z - shift) % Z * C + 1))
    return pairs


def across(shift):
    pairs = []
    for z in range(Z):
        pairs.append((z * C, (z - shift) % Z * C + 1))
        pairs.append((z * C + 1, (z + shift) % Z * C))
    return pairs


def send(value, shift):
    return lax.ppermute(value, ("s", "c"), along(shift))


def back_across(value, shift):
    return lax.ppermute(value, ("s", "c"), across(shift))


def swap(value):
    return lax.ppermute(value, "c", [(0, 1), (1, 0)])


def extend_kernel(tokens, ids, gates, out):
    block, width = tokens.shape
    gate = gates[...]
    high = gate.astype(BF)
    rest = gate - high.astype(F32)
    middle = rest.astype(BF)
    low = (rest - middle.astype(F32)).astype(BF)
    parts = [v.astype(F32) for v in (ids[...], high, middle, low)]
    used = sum(p.shape[0] for p in parts)
    parts.append(jnp.zeros((TAIL - used, block), F32))
    table = jnp.concatenate(parts, axis=0).astype(BF)
    left = lax.broadcasted_iota(jnp.int32, (block, block), 0)
    right = lax.broadcasted_iota(jnp.int32, (block, block), 1)
    unit = jnp.where(left == right, 1.0, 0.0).astype(BF)
    tail = lax.dot_general(unit, table, (((1,), (1,)), ((), ())), preferred_element_type=F32)
    out[:, :width] = tokens[...]
    out[:, width:] = tail.astype(BF)


def extend(tokens, expert_ids, gates):
    block, width = tokens.shape
    return pl.pallas_call(
        extend_kernel,
        out_shape=jax.ShapeDtypeStruct((block, width + TAIL), BF),
        compiler_params=pltpu.CompilerParams(vmem_limit_bytes=4 * MIB),
        name="extend",
    )(*[pltpu.with_memory_space_constraint(v, pltpu.HBM) for v in (tokens, expert_ids.T, gates.T)])


def place_kernel(block, *refs):
    pieces, (rows_out, high_out, low_out) = list(refs[:-3]), refs[-3:]
    pieces[0] = pieces[0].at[:block]
    width = rows_out.shape[1]
    rows = sum(p.shape[0] for p in pieces)
    blocks = rows // block
    per_expert = blocks * SLOTS
    slots = PLANE * per_expert
    tail = [p[:, width:].astype(F32) for p in pieces]
    if rows < TAIL:
        tail.append(jnp.zeros((TAIL - rows, TAIL), F32))
    tail = jnp.concatenate(tail, axis=0).T[:, :rows]
    peer = lax.broadcasted_iota(jnp.int32, (PLANE, rows), 0)
    peer = (peer // Y % PAIR * Y + peer % Y) * X + peer // (Y * PAIR)
    expert = (lax.axis_index("s") * PLANE + peer).astype(F32)
    named = jnp.zeros((PLANE, rows), F32)
    gate = jnp.zeros((PLANE, rows), F32)
    for k in range(8):
        hit = tail[k : k + 1] == expert
        value = tail[8 + k : 9 + k] + tail[16 + k : 17 + k] + tail[24 + k : 25 + k]
        named = named + jnp.where(hit, 1.0, 0.0)
        gate = gate + jnp.where(hit, value, 0.0)
    before = lax.broadcasted_iota(jnp.int32, (rows, rows), 0)
    after = lax.broadcasted_iota(jnp.int32, (rows, rows), 1)
    earlier = jnp.where((before < after) & (before // block == after // block), 1.0, 0.0).astype(BF)
    rank = jnp.dot(named.astype(BF), earlier, preferred_element_type=F32)

    def spread(value):
        return jnp.broadcast_to(value[:, None, :], (PLANE, per_expert, rows)).reshape(slots, rows)

    slot = lax.broadcasted_iota(jnp.int32, (slots, rows), 0)
    lane = lax.broadcasted_iota(jnp.int32, (slots, rows), 1)
    here = (slot // SLOTS) % blocks == lane // block
    chosen = here & (spread(named) > 0.5) & (spread(rank) == (slot % SLOTS).astype(F32))
    weight = jnp.where(chosen, spread(gate), 0.0)
    high = weight.astype(BF)
    high_out[...] = high
    low_out[...] = (weight - high.astype(F32)).astype(BF)
    pick = jnp.where(chosen, 1.0, 0.0).astype(BF)
    step = 512
    for c in range(0, width, step):
        part = jnp.concatenate([p[:, c : c + step] for p in pieces], axis=0)
        rows_out[:, c : c + step] = jnp.dot(pick, part, preferred_element_type=F32).astype(BF)


def place(pieces, block, width):
    rows = sum(p.shape[0] for p in pieces) - block
    slots = PLANE * SLOTS * (rows // block)

    def kernel(*refs):
        place_kernel(block, *refs)

    return pl.pallas_call(
        kernel,
        out_shape=(
            jax.ShapeDtypeStruct((slots, width), BF),
            jax.ShapeDtypeStruct((slots, rows), BF),
            jax.ShapeDtypeStruct((slots, rows), BF),
        ),
        compiler_params=pltpu.CompilerParams(vmem_limit_bytes=16 * MIB),
        cost_estimate=pl.CostEstimate(flops=2 * slots * rows * width, bytes_accessed=2 * (slots + rows) * width, transcendentals=0),
        name="place",
    )(*pieces)


def expert_kernel(rows, gate_a, up_a, down_a, gate_b, up_b, down_b, out, gate_v, up_v, down_v, hidden, sems):
    half = gate_a.shape[1]
    width = out.shape[1]
    pairs = ((gate_a, gate_v), (up_a, up_v), (down_a, down_v))
    copies = [pltpu.make_async_copy(src, dst, sems.at[i]) for i, (src, dst) in enumerate(pairs)]
    for copy in copies:
        copy.start()
    tile = 256
    for h, (gate, up) in enumerate(((gate_b, up_b), (gate_v, up_v))):
        if h == 1:
            copies[0].wait()
            copies[1].wait()
        for j in range(0, half, tile):
            g = jnp.dot(rows[...], gate[:, j : j + tile], preferred_element_type=F32)
            u = jnp.dot(rows[...], up[:, j : j + tile], preferred_element_type=F32)
            hidden[:, h * half + j : h * half + j + tile] = (g / (1.0 + jnp.exp(-g)) * u).astype(BF)
    copies[2].wait()
    for c in range(0, width, tile):
        total = jnp.dot(hidden[:, :half], down_b[:, c : c + tile], preferred_element_type=F32)
        total = total + jnp.dot(hidden[:, half:], down_v[:, c : c + tile], preferred_element_type=F32)
        out[:, c : c + tile] = total.astype(BF)


def experts(rows, own, other):
    width, half = own[0].shape
    count = rows.shape[0]
    return pl.pallas_call(
        expert_kernel,
        out_shape=jax.ShapeDtypeStruct(rows.shape, BF),
        in_specs=[VMEM] + [pl.BlockSpec(memory_space=pl.ANY)] * 3 + [VMEM] * 3,
        out_specs=VMEM,
        scratch_shapes=[
            pltpu.VMEM((width, half), BF),
            pltpu.VMEM((width, half), BF),
            pltpu.VMEM((half, width), BF),
            pltpu.VMEM((count, 2 * half), BF),
            pltpu.SemaphoreType.DMA((3,)),
        ],
        compiler_params=pltpu.CompilerParams(vmem_limit_bytes=32 * MIB),
        cost_estimate=pl.CostEstimate(
            flops=2 * count * width * half * 6, bytes_accessed=12 * width * half + 4 * count * width, transcendentals=2 * count * half
        ),
        name="experts",
    )(rows, *own, *other)


def collect_kernel(returned, high, low, *outs):
    step = 512
    over = (((0,), (0,)), ((), ()))
    for c in range(0, returned.shape[1], step):
        part = returned[:, c : c + step]
        total = lax.dot_general(high[...], part, over, preferred_element_type=F32)
        total = total + lax.dot_general(low[...], part, over, preferred_element_type=F32)
        start = 0
        for out in outs:
            count = out.shape[0]
            out[:, c : c + step] = total[start : start + count].astype(out.dtype)
            start += count


def collect(returned, high, low, shapes):
    slots, width = returned.shape
    rows = high.shape[1]
    return pl.pallas_call(
        collect_kernel,
        out_shape=[jax.ShapeDtypeStruct((count, width), kind) for count, kind in shapes],
        compiler_params=pltpu.CompilerParams(vmem_limit_bytes=16 * MIB),
        cost_estimate=pl.CostEstimate(flops=4 * slots * rows * width, bytes_accessed=2 * (slots + rows) * width, transcendentals=0),
        name="collect",
    )(returned, high, low)


def exchange(value):
    width = value.shape[1]
    return lax.all_to_all(value.reshape(PLANE, -1, width), ("x", "p", "y"), 0, 0, tiled=True).reshape(-1, width)


def body(tokens, expert_ids, gates, gate_weight, up_weight, down_weight):
    block, width = tokens.shape
    own_weights = [gate_weight[0], up_weight[0], down_weight[0]]
    own = extend(tokens, expert_ids, gates)
    other, sent_weights = lax.optimization_barrier((swap(own), own_weights[1:]))
    other_weights = [swap(w) for w in own_weights[:1] + sent_weights]
    own_weights = [pltpu.with_memory_space_constraint(w, pltpu.HBM) for w in own_weights]

    both = jnp.concatenate([own, other], axis=0)
    far = send(own, 2)
    near = send(both, 1)
    rows, high, low = place((both, near, far), block, width)
    rows, other_weights = lax.optimization_barrier((rows, other_weights))
    other_weights = [pltpu.with_memory_space_constraint(w, pltpu.VMEM) for w in other_weights]
    done = experts(exchange(rows), own_weights, other_weights)
    returned = exchange(done)
    shapes = ((block, F32), (block, BF), (block, BF), (block, BF))
    q_own, q_near, q_near_other, q_far = collect(returned, high, low, shapes)
    far = send(q_far, -2)
    near = send(q_near, -1)
    near_other = back_across(q_near_other, 1)
    return (q_own + near.astype(F32) + near_other.astype(F32) + far.astype(F32)).astype(BF)


def solution(mesh):
    names = ("s", "p", "y", "x", "c")
    fine = Mesh(mesh.devices.reshape(Z, PAIR, Y, X, C), names)
    rows = P(names)
    return jax.shard_map(body, mesh=fine, in_specs=(rows,) * 6, out_specs=rows, check_vma=False)
```

```python
import jax
import jax.numpy as jnp
from jax import lax
from jax.experimental import pallas as pl
from jax.experimental.pallas import tpu as pltpu
from jax.sharding import Mesh, PartitionSpec as P

Z, PAIR, Y, X, C = 4, 2, 4, 4, 2
PLANE = PAIR * Y * X
SLOTS = 2
TAIL = 128
BF = jnp.bfloat16
F32 = jnp.float32
MIB = 1 << 20
VMEM = pl.BlockSpec(memory_space=pltpu.VMEM)


def along(shift):
    pairs = []
    for z in range(Z):
        pairs.append((z * C, (z + shift) % Z * C))
        pairs.append((z * C + 1, (z - shift) % Z * C + 1))
    return pairs


def across(shift):
    pairs = []
    for z in range(Z):
        pairs.append((z * C, (z - shift) % Z * C + 1))
        pairs.append((z * C + 1, (z + shift) % Z * C))
    return pairs


def send(value, shift):
    return lax.ppermute(value, ("s", "c"), along(shift))


def back_across(value, shift):
    return lax.ppermute(value, ("s", "c"), across(shift))


def swap(value):
    return lax.ppermute(value, "c", [(0, 1), (1, 0)])


def extend_kernel(tokens, ids, gates, out):
    block, width = tokens.shape
    gate = gates[...]
    high = gate.astype(BF)
    rest = gate - high.astype(F32)
    middle = rest.astype(BF)
    low = (rest - middle.astype(F32)).astype(BF)
    parts = [v.astype(F32) for v in (ids[...], high, middle, low)]
    used = sum(p.shape[0] for p in parts)
    parts.append(jnp.zeros((TAIL - used, block), F32))
    table = jnp.concatenate(parts, axis=0).astype(BF)
    left = lax.broadcasted_iota(jnp.int32, (block, block), 0)
    right = lax.broadcasted_iota(jnp.int32, (block, block), 1)
    unit = jnp.where(left == right, 1.0, 0.0).astype(BF)
    tail = lax.dot_general(unit, table, (((1,), (1,)), ((), ())), preferred_element_type=F32)
    out[:, :width] = tokens[...]
    out[:, width:] = tail.astype(BF)


def extend(tokens, expert_ids, gates):
    block, width = tokens.shape
    return pl.pallas_call(
        extend_kernel,
        out_shape=jax.ShapeDtypeStruct((block, width + TAIL), BF),
        compiler_params=pltpu.CompilerParams(vmem_limit_bytes=4 * MIB),
        name="extend",
    )(*[pltpu.with_memory_space_constraint(v, pltpu.HBM) for v in (tokens, expert_ids.T, gates.T)])


def place_kernel(block, *refs):
    pieces, (rows_out, high_out, low_out) = list(refs[:-3]), refs[-3:]
    pieces[0] = pieces[0].at[:block]
    width = rows_out.shape[1]
    rows = sum(p.shape[0] for p in pieces)
    blocks = rows // block
    per_expert = blocks * SLOTS
    slots = PLANE * per_expert
    tail = [p[:, width:].astype(F32) for p in pieces]
    if rows < TAIL:
        tail.append(jnp.zeros((TAIL - rows, TAIL), F32))
    tail = jnp.concatenate(tail, axis=0).T[:, :rows]
    peer = lax.broadcasted_iota(jnp.int32, (PLANE, rows), 0)
    peer = peer + lax.axis_index("c") * (PLANE - 1 - 2 * peer)
    peer = (peer // Y % PAIR * Y + peer % Y) * X + peer // (Y * PAIR)
    expert = (lax.axis_index("s") * PLANE + peer).astype(F32)
    named = jnp.zeros((PLANE, rows), F32)
    gate = jnp.zeros((PLANE, rows), F32)
    for k in range(8):
        hit = tail[k : k + 1] == expert
        value = tail[8 + k : 9 + k] + tail[16 + k : 17 + k] + tail[24 + k : 25 + k]
        named = named + jnp.where(hit, 1.0, 0.0)
        gate = gate + jnp.where(hit, value, 0.0)
    before = lax.broadcasted_iota(jnp.int32, (rows, rows), 0)
    after = lax.broadcasted_iota(jnp.int32, (rows, rows), 1)
    earlier = jnp.where((before < after) & (before // block == after // block), 1.0, 0.0).astype(BF)
    rank = jnp.dot(named.astype(BF), earlier, preferred_element_type=F32)

    def spread(value):
        return jnp.broadcast_to(value[:, None, :], (PLANE, per_expert, rows)).reshape(slots, rows)

    slot = lax.broadcasted_iota(jnp.int32, (slots, rows), 0)
    lane = lax.broadcasted_iota(jnp.int32, (slots, rows), 1)
    here = (slot // SLOTS) % blocks == lane // block
    chosen = here & (spread(named) > 0.5) & (spread(rank) == (slot % SLOTS).astype(F32))
    weight = jnp.where(chosen, spread(gate), 0.0)
    high = weight.astype(BF)
    high_out[...] = high
    low_out[...] = (weight - high.astype(F32)).astype(BF)
    pick = jnp.where(chosen, 1.0, 0.0).astype(BF)
    step = 512
    for c in range(0, width, step):
        part = jnp.concatenate([p[:, c : c + step] for p in pieces], axis=0)
        rows_out[:, c : c + step] = jnp.dot(pick, part, preferred_element_type=F32).astype(BF)


def place(pieces, block, width):
    rows = sum(p.shape[0] for p in pieces) - block
    slots = PLANE * SLOTS * (rows // block)

    def kernel(*refs):
        place_kernel(block, *refs)

    return pl.pallas_call(
        kernel,
        out_shape=(
            jax.ShapeDtypeStruct((slots, width), BF),
            jax.ShapeDtypeStruct((slots, rows), BF),
            jax.ShapeDtypeStruct((slots, rows), BF),
        ),
        compiler_params=pltpu.CompilerParams(vmem_limit_bytes=16 * MIB),
        cost_estimate=pl.CostEstimate(flops=2 * slots * rows * width, bytes_accessed=2 * (slots + rows) * width, transcendentals=0),
        name="place",
    )(*pieces)


def expert_kernel(rows, gate_a, up_a, down_a, gate_b, up_b, down_b, out, gate_v, up_v, down_v, hidden, sems):
    half = gate_a.shape[1]
    width = out.shape[1]
    pairs = ((gate_a, gate_v), (up_a, up_v), (down_a, down_v))
    copies = [pltpu.make_async_copy(src, dst, sems.at[i]) for i, (src, dst) in enumerate(pairs)]
    for copy in copies:
        copy.start()
    tile = 256
    for h, (gate, up) in enumerate(((gate_b, up_b), (gate_v, up_v))):
        if h == 1:
            copies[0].wait()
            copies[1].wait()
        for j in range(0, half, tile):
            g = jnp.dot(rows[...], gate[:, j : j + tile], preferred_element_type=F32)
            u = jnp.dot(rows[...], up[:, j : j + tile], preferred_element_type=F32)
            hidden[:, h * half + j : h * half + j + tile] = (g / (1.0 + jnp.exp(-g)) * u).astype(BF)
    copies[2].wait()
    for c in range(0, width, tile):
        total = jnp.dot(hidden[:, :half], down_b[:, c : c + tile], preferred_element_type=F32)
        total = total + jnp.dot(hidden[:, half:], down_v[:, c : c + tile], preferred_element_type=F32)
        out[:, c : c + tile] = total.astype(BF)


def experts(rows, own, other):
    width, half = own[0].shape
    count = rows.shape[0]
    return pl.pallas_call(
        expert_kernel,
        out_shape=jax.ShapeDtypeStruct(rows.shape, BF),
        in_specs=[VMEM] + [pl.BlockSpec(memory_space=pl.ANY)] * 3 + [VMEM] * 3,
        out_specs=VMEM,
        scratch_shapes=[
            pltpu.VMEM((width, half), BF),
            pltpu.VMEM((width, half), BF),
            pltpu.VMEM((half, width), BF),
            pltpu.VMEM((count, 2 * half), BF),
            pltpu.SemaphoreType.DMA((3,)),
        ],
        compiler_params=pltpu.CompilerParams(vmem_limit_bytes=32 * MIB),
        cost_estimate=pl.CostEstimate(
            flops=2 * count * width * half * 6, bytes_accessed=12 * width * half + 4 * count * width, transcendentals=2 * count * half
        ),
        name="experts",
    )(rows, *own, *other)


def collect_kernel(returned, high, low, *outs):
    step = 512
    over = (((0,), (0,)), ((), ()))
    for c in range(0, returned.shape[1], step):
        part = returned[:, c : c + step]
        total = lax.dot_general(high[...], part, over, preferred_element_type=F32)
        total = total + lax.dot_general(low[...], part, over, preferred_element_type=F32)
        start = 0
        for out in outs:
            count = out.shape[0]
            out[:, c : c + step] = total[start : start + count].astype(out.dtype)
            start += count


def collect(returned, high, low, shapes):
    slots, width = returned.shape
    rows = high.shape[1]
    return pl.pallas_call(
        collect_kernel,
        out_shape=[jax.ShapeDtypeStruct((count, width), kind) for count, kind in shapes],
        compiler_params=pltpu.CompilerParams(vmem_limit_bytes=16 * MIB),
        cost_estimate=pl.CostEstimate(flops=4 * slots * rows * width, bytes_accessed=2 * (slots + rows) * width, transcendentals=0),
        name="collect",
    )(returned, high, low)


def groups():
    out = []
    for s in range(Z):
        for c in range(C):
            chips = [(p, y, x) for x in range(X) for p in range(PAIR) for y in range(Y)]
            if c == 1:
                chips = chips[::-1]
            out.append([(((s * PAIR + p) * Y + y) * X + x) * C + c for p, y, x in chips])
    return out


def exchange(value):
    width = value.shape[1]
    blocks = value.reshape(PLANE, -1, width)
    names = ("s", "p", "y", "x", "c")
    return lax.all_to_all(blocks, names, 0, 0, axis_index_groups=groups(), tiled=True).reshape(-1, width)


def body(tokens, expert_ids, gates, gate_weight, up_weight, down_weight):
    block, width = tokens.shape
    own_weights = [gate_weight[0], up_weight[0], down_weight[0]]
    own = extend(tokens, expert_ids, gates)
    other, sent_weights = lax.optimization_barrier((swap(own), own_weights[1:]))
    other_weights = [swap(w) for w in own_weights[:1] + sent_weights]
    own_weights = [pltpu.with_memory_space_constraint(w, pltpu.HBM) for w in own_weights]

    both = jnp.concatenate([own, other], axis=0)
    far = send(own, 2)
    near = send(both, 1)
    rows, high, low = place((both, near, far), block, width)
    rows, other_weights = lax.optimization_barrier((rows, other_weights))
    other_weights = [pltpu.with_memory_space_constraint(w, pltpu.VMEM) for w in other_weights]
    done = experts(exchange(rows), own_weights, other_weights)
    returned = exchange(done)
    shapes = ((block, F32), (block, BF), (block, BF), (block, BF))
    q_own, q_near, q_near_other, q_far = collect(returned, high, low, shapes)
    far = send(q_far, -2)
    near = send(q_near, -1)
    near_other = back_across(q_near_other, 1)
    return (q_own + near.astype(F32) + near_other.astype(F32) + far.astype(F32)).astype(BF)


def solution(mesh):
    names = ("s", "p", "y", "x", "c")
    fine = Mesh(mesh.devices.reshape(Z, PAIR, Y, X, C), names)
    rows = P(names)
    return jax.shard_map(body, mesh=fine, in_specs=(rows,) * 6, out_specs=rows, check_vma=False)
```

```python
import jax
import jax.numpy as jnp
from jax import lax
from jax.experimental import pallas as pl
from jax.experimental.pallas import tpu as pltpu
from jax.sharding import Mesh, PartitionSpec as P

Z, PAIR, Y, X, C = 4, 2, 4, 4, 2
PLANE = PAIR * Y * X
SLOTS = 2
TAIL = 128
BF = jnp.bfloat16
F32 = jnp.float32
MIB = 1 << 20
VMEM = pl.BlockSpec(memory_space=pltpu.VMEM)


def along(shift):
    pairs = []
    for z in range(Z):
        pairs.append((z * C, (z + shift) % Z * C))
        pairs.append((z * C + 1, (z - shift) % Z * C + 1))
    return pairs


def across(shift):
    pairs = []
    for z in range(Z):
        pairs.append((z * C, (z - shift) % Z * C + 1))
        pairs.append((z * C + 1, (z + shift) % Z * C))
    return pairs


def send(value, shift):
    return lax.ppermute(value, ("s", "c"), along(shift))


def back_across(value, shift):
    return lax.ppermute(value, ("s", "c"), across(shift))


def swap(value):
    return lax.ppermute(value, "c", [(0, 1), (1, 0)])


def extend_kernel(tokens, ids, gates, out):
    block, width = tokens.shape
    gate = gates[...]
    high = gate.astype(BF)
    rest = gate - high.astype(F32)
    middle = rest.astype(BF)
    low = (rest - middle.astype(F32)).astype(BF)
    parts = [v.astype(F32) for v in (ids[...], high, middle, low)]
    used = sum(p.shape[0] for p in parts)
    parts.append(jnp.zeros((TAIL - used, block), F32))
    table = jnp.concatenate(parts, axis=0).astype(BF)
    left = lax.broadcasted_iota(jnp.int32, (block, block), 0)
    right = lax.broadcasted_iota(jnp.int32, (block, block), 1)
    unit = jnp.where(left == right, 1.0, 0.0).astype(BF)
    tail = lax.dot_general(unit, table, (((1,), (1,)), ((), ())), preferred_element_type=F32)
    out[:, :width] = tokens[...]
    out[:, width:] = tail.astype(BF)


def extend(tokens, expert_ids, gates):
    block, width = tokens.shape
    return pl.pallas_call(
        extend_kernel,
        out_shape=jax.ShapeDtypeStruct((block, width + TAIL), BF),
        compiler_params=pltpu.CompilerParams(vmem_limit_bytes=4 * MIB),
        name="extend",
    )(*[pltpu.with_memory_space_constraint(v, pltpu.HBM) for v in (tokens, expert_ids.T, gates.T)])


def place_kernel(block, *refs):
    pieces, (rows_out, high_out, low_out) = list(refs[:-3]), refs[-3:]
    pieces[0] = pieces[0].at[:block]
    width = rows_out.shape[1]
    rows = sum(p.shape[0] for p in pieces)
    blocks = rows // block
    per_expert = blocks * SLOTS
    slots = PLANE * per_expert
    tail = [p[:, width:].astype(F32) for p in pieces]
    if rows < TAIL:
        tail.append(jnp.zeros((TAIL - rows, TAIL), F32))
    tail = jnp.concatenate(tail, axis=0).T[:, :rows]
    peer = lax.broadcasted_iota(jnp.int32, (PLANE, rows), 0)
    peer = peer + lax.axis_index("c") * (PLANE - 1 - 2 * peer)
    peer = (peer // Y % PAIR * Y + peer % Y) * X + peer // (Y * PAIR)
    expert = (lax.axis_index("s") * PLANE + peer).astype(F32)
    named = jnp.zeros((PLANE, rows), F32)
    gate = jnp.zeros((PLANE, rows), F32)
    for k in range(8):
        hit = tail[k : k + 1] == expert
        value = tail[8 + k : 9 + k] + tail[16 + k : 17 + k] + tail[24 + k : 25 + k]
        named = named + jnp.where(hit, 1.0, 0.0)
        gate = gate + jnp.where(hit, value, 0.0)
    before = lax.broadcasted_iota(jnp.int32, (rows, rows), 0)
    after = lax.broadcasted_iota(jnp.int32, (rows, rows), 1)
    earlier = jnp.where((before < after) & (before // block == after // block), 1.0, 0.0).astype(BF)
    rank = jnp.dot(named.astype(BF), earlier, preferred_element_type=F32)

    def spread(value):
        return jnp.broadcast_to(value[:, None, :], (PLANE, per_expert, rows)).reshape(slots, rows)

    slot = lax.broadcasted_iota(jnp.int32, (slots, rows), 0)
    lane = lax.broadcasted_iota(jnp.int32, (slots, rows), 1)
    here = (slot // SLOTS) % blocks == lane // block
    chosen = here & (spread(named) > 0.5) & (spread(rank) == (slot % SLOTS).astype(F32))
    weight = jnp.where(chosen, spread(gate), 0.0)
    high = weight.astype(BF)
    high_out[...] = high
    low_out[...] = (weight - high.astype(F32)).astype(BF)
    pick = jnp.where(chosen, 1.0, 0.0).astype(BF)
    step = 512
    for c in range(0, width, step):
        part = jnp.concatenate([p[:, c : c + step] for p in pieces], axis=0)
        rows_out[:, c : c + step] = jnp.dot(pick, part, preferred_element_type=F32).astype(BF)


def place(pieces, block, width):
    rows = sum(p.shape[0] for p in pieces) - block
    slots = PLANE * SLOTS * (rows // block)

    def kernel(*refs):
        place_kernel(block, *refs)

    return pl.pallas_call(
        kernel,
        out_shape=(
            jax.ShapeDtypeStruct((slots, width), BF),
            jax.ShapeDtypeStruct((slots, rows), BF),
            jax.ShapeDtypeStruct((slots, rows), BF),
        ),
        compiler_params=pltpu.CompilerParams(vmem_limit_bytes=16 * MIB),
        cost_estimate=pl.CostEstimate(flops=2 * slots * rows * width, bytes_accessed=2 * (slots + rows) * width, transcendentals=0),
        name="place",
    )(*pieces)


def expert_kernel(rows, gate_a, up_a, down_a, gate_b, up_b, down_b, out, gate_v, up_v, down_v, hidden, sems):
    half = gate_a.shape[1]
    width = out.shape[1]
    pairs = ((gate_a, gate_v), (up_a, up_v), (down_a, down_v))
    copies = [pltpu.make_async_copy(src, dst, sems.at[i]) for i, (src, dst) in enumerate(pairs)]
    for copy in copies:
        copy.start()
    tile = 256
    for h, (gate, up) in enumerate(((gate_b, up_b), (gate_v, up_v))):
        if h == 1:
            copies[0].wait()
            copies[1].wait()
        for j in range(0, half, tile):
            g = jnp.dot(rows[...], gate[:, j : j + tile], preferred_element_type=F32)
            u = jnp.dot(rows[...], up[:, j : j + tile], preferred_element_type=F32)
            hidden[:, h * half + j : h * half + j + tile] = (g / (1.0 + jnp.exp(-g)) * u).astype(BF)
    copies[2].wait()
    for c in range(0, width, tile):
        total = jnp.dot(hidden[:, :half], down_b[:, c : c + tile], preferred_element_type=F32)
        total = total + jnp.dot(hidden[:, half:], down_v[:, c : c + tile], preferred_element_type=F32)
        out[:, c : c + tile] = total.astype(BF)


def experts(rows, own, other):
    width, half = own[0].shape
    count = rows.shape[0]
    return pl.pallas_call(
        expert_kernel,
        out_shape=jax.ShapeDtypeStruct(rows.shape, BF),
        in_specs=[VMEM] + [pl.BlockSpec(memory_space=pl.ANY)] * 3 + [VMEM] * 3,
        out_specs=VMEM,
        scratch_shapes=[
            pltpu.VMEM((width, half), BF),
            pltpu.VMEM((width, half), BF),
            pltpu.VMEM((half, width), BF),
            pltpu.VMEM((count, 2 * half), BF),
            pltpu.SemaphoreType.DMA((3,)),
        ],
        compiler_params=pltpu.CompilerParams(vmem_limit_bytes=32 * MIB),
        cost_estimate=pl.CostEstimate(
            flops=2 * count * width * half * 6, bytes_accessed=12 * width * half + 4 * count * width, transcendentals=2 * count * half
        ),
        name="experts",
    )(rows, *own, *other)


def collect_kernel(returned, high, low, *outs):
    step = 512
    over = (((0,), (0,)), ((), ()))
    for c in range(0, returned.shape[1], step):
        part = returned[:, c : c + step]
        total = lax.dot_general(high[...], part, over, preferred_element_type=F32)
        total = total + lax.dot_general(low[...], part, over, preferred_element_type=F32)
        start = 0
        for out in outs:
            count = out.shape[0]
            out[:, c : c + step] = total[start : start + count].astype(out.dtype)
            start += count


def collect(returned, high, low, shapes):
    slots, width = returned.shape
    rows = high.shape[1]
    return pl.pallas_call(
        collect_kernel,
        out_shape=[jax.ShapeDtypeStruct((count, width), kind) for count, kind in shapes],
        compiler_params=pltpu.CompilerParams(vmem_limit_bytes=16 * MIB),
        cost_estimate=pl.CostEstimate(flops=4 * slots * rows * width, bytes_accessed=2 * (slots + rows) * width, transcendentals=0),
        name="collect",
    )(returned, high, low)


def groups():
    out = []
    for s in range(Z):
        for c in range(C):
            chips = [(p, y, x) for x in range(X) for p in range(PAIR) for y in range(Y)]
            if c == 1:
                chips = chips[::-1]
            out.append([(((s * PAIR + p) * Y + y) * X + x) * C + c for p, y, x in chips])
    return out


def exchange(value):
    width = value.shape[1]
    blocks = value.reshape(PLANE, -1, width)
    names = ("s", "p", "y", "x", "c")
    return lax.all_to_all(blocks, names, 0, 0, axis_index_groups=groups(), tiled=True).reshape(-1, width)


def body(tokens, expert_ids, gates, gate_weight, up_weight, down_weight):
    block, width = tokens.shape
    own_weights = [gate_weight[0], up_weight[0], down_weight[0]]
    own = extend(tokens, expert_ids, gates)
    other, sent_weights = lax.optimization_barrier((swap(own), own_weights[1:]))
    other_weights = [swap(w) for w in own_weights[:1] + sent_weights]
    own_weights[1:] = [pltpu.with_memory_space_constraint(w, pltpu.HBM) for w in own_weights[1:]]

    both = jnp.concatenate([own, other], axis=0)
    far = send(own, 2)
    near = send(both, 1)
    rows, high, low = place((both, near, far), block, width)
    rows, other_weights = lax.optimization_barrier((rows, other_weights))
    other_weights = [pltpu.with_memory_space_constraint(w, pltpu.VMEM) for w in other_weights]
    done = experts(exchange(rows), own_weights, other_weights)
    returned = exchange(done)
    shapes = ((block, F32), (block, F32), (block, BF), (block, BF))
    q_own, q_near, q_near_other, q_far = collect(returned, high, low, shapes)
    far = send(q_far, -1)
    near_other = back_across(q_near_other, 1)
    near = send((q_near + far.astype(F32)).astype(BF), -1)
    return (q_own + near_other.astype(F32) + near.astype(F32)).astype(BF)


def solution(mesh):
    names = ("s", "p", "y", "x", "c")
    fine = Mesh(mesh.devices.reshape(Z, PAIR, Y, X, C), names)
    rows = P(names)
    return jax.shard_map(body, mesh=fine, in_specs=(rows,) * 6, out_specs=rows, check_vma=False)
```

```python
import jax
import jax.numpy as jnp
from jax import lax
from jax.experimental import pallas as pl
from jax.experimental.pallas import tpu as pltpu
from jax.sharding import Mesh, PartitionSpec as P

Z, PAIR, Y, X, C = 4, 2, 4, 4, 2
PLANE = PAIR * Y * X
SLOTS = 2
TAIL = 128
BF = jnp.bfloat16
F32 = jnp.float32
MIB = 1 << 20
VMEM = pl.BlockSpec(memory_space=pltpu.VMEM)


def along(shift):
    pairs = []
    for z in range(Z):
        pairs.append((z * C, (z + shift) % Z * C))
        pairs.append((z * C + 1, (z - shift) % Z * C + 1))
    return pairs


def across(shift):
    pairs = []
    for z in range(Z):
        pairs.append((z * C, (z - shift) % Z * C + 1))
        pairs.append((z * C + 1, (z + shift) % Z * C))
    return pairs


def send(value, shift):
    return lax.ppermute(value, ("s", "c"), along(shift))


def back_across(value, shift):
    return lax.ppermute(value, ("s", "c"), across(shift))


def swap(value):
    return lax.ppermute(value, "c", [(0, 1), (1, 0)])


def extend_kernel(tokens, ids, gates, out):
    block, width = tokens.shape
    gate = gates[...]
    high = gate.astype(BF)
    rest = gate - high.astype(F32)
    middle = rest.astype(BF)
    low = (rest - middle.astype(F32)).astype(BF)
    parts = [v.astype(F32) for v in (ids[...], high, middle, low)]
    used = sum(p.shape[0] for p in parts)
    parts.append(jnp.zeros((TAIL - used, block), F32))
    table = jnp.concatenate(parts, axis=0).astype(BF)
    left = lax.broadcasted_iota(jnp.int32, (block, block), 0)
    right = lax.broadcasted_iota(jnp.int32, (block, block), 1)
    unit = jnp.where(left == right, 1.0, 0.0).astype(BF)
    tail = lax.dot_general(unit, table, (((1,), (1,)), ((), ())), preferred_element_type=F32)
    out[:, :width] = tokens[...]
    out[:, width:] = tail.astype(BF)


def extend(tokens, expert_ids, gates):
    block, width = tokens.shape
    return pl.pallas_call(
        extend_kernel,
        out_shape=jax.ShapeDtypeStruct((block, width + TAIL), BF),
        compiler_params=pltpu.CompilerParams(vmem_limit_bytes=4 * MIB),
        name="extend",
    )(*[pltpu.with_memory_space_constraint(v, pltpu.HBM) for v in (tokens, expert_ids.T, gates.T)])


def place_kernel(block, *refs):
    pieces, (rows_out, high_out, low_out) = list(refs[:-3]), refs[-3:]
    pieces[0] = pieces[0].at[:block]
    width = rows_out.shape[1]
    rows = sum(p.shape[0] for p in pieces)
    blocks = rows // block
    per_expert = blocks * SLOTS
    slots = PLANE * per_expert
    tail = [p[:, width:].astype(F32) for p in pieces]
    if rows < TAIL:
        tail.append(jnp.zeros((TAIL - rows, TAIL), F32))
    tail = jnp.concatenate(tail, axis=0).T[:, :rows]
    peer = lax.broadcasted_iota(jnp.int32, (PLANE, rows), 0)
    peer = peer + lax.axis_index("c") * (PLANE - 1 - 2 * peer)
    peer = (peer // Y % PAIR * Y + peer % Y) * X + peer // (Y * PAIR)
    expert = (lax.axis_index("s") * PLANE + peer).astype(F32)
    named = jnp.zeros((PLANE, rows), F32)
    gate = jnp.zeros((PLANE, rows), F32)
    for k in range(8):
        hit = tail[k : k + 1] == expert
        value = tail[8 + k : 9 + k] + tail[16 + k : 17 + k] + tail[24 + k : 25 + k]
        named = named + jnp.where(hit, 1.0, 0.0)
        gate = gate + jnp.where(hit, value, 0.0)
    before = lax.broadcasted_iota(jnp.int32, (rows, rows), 0)
    after = lax.broadcasted_iota(jnp.int32, (rows, rows), 1)
    earlier = jnp.where((before < after) & (before // block == after // block), 1.0, 0.0).astype(BF)
    rank = jnp.dot(named.astype(BF), earlier, preferred_element_type=F32)

    def spread(value):
        return jnp.broadcast_to(value[:, None, :], (PLANE, per_expert, rows)).reshape(slots, rows)

    slot = lax.broadcasted_iota(jnp.int32, (slots, rows), 0)
    lane = lax.broadcasted_iota(jnp.int32, (slots, rows), 1)
    here = (slot // SLOTS) % blocks == lane // block
    chosen = here & (spread(named) > 0.5) & (spread(rank) == (slot % SLOTS).astype(F32))
    weight = jnp.where(chosen, spread(gate), 0.0)
    high = weight.astype(BF)
    high_out[...] = high
    low_out[...] = (weight - high.astype(F32)).astype(BF)
    pick = jnp.where(chosen, 1.0, 0.0).astype(BF)
    step = 512
    for c in range(0, width, step):
        part = jnp.concatenate([p[:, c : c + step] for p in pieces], axis=0)
        rows_out[:, c : c + step] = jnp.dot(pick, part, preferred_element_type=F32).astype(BF)


def place(pieces, block, width):
    rows = sum(p.shape[0] for p in pieces) - block
    slots = PLANE * SLOTS * (rows // block)

    def kernel(*refs):
        place_kernel(block, *refs)

    return pl.pallas_call(
        kernel,
        out_shape=(
            jax.ShapeDtypeStruct((slots, width), BF),
            jax.ShapeDtypeStruct((slots, rows), BF),
            jax.ShapeDtypeStruct((slots, rows), BF),
        ),
        compiler_params=pltpu.CompilerParams(vmem_limit_bytes=16 * MIB),
        cost_estimate=pl.CostEstimate(flops=2 * slots * rows * width, bytes_accessed=2 * (slots + rows) * width, transcendentals=0),
        name="place",
    )(*pieces)


def expert_kernel(rows, gate_a, up_a, down_a, gate_b, up_b, down_b, out, gate_v, up_v, down_v, hidden, sems):
    half = gate_a.shape[1]
    width = out.shape[1]
    pairs = ((gate_a, gate_v), (up_a, up_v), (down_a, down_v))
    copies = [pltpu.make_async_copy(src, dst, sems.at[i]) for i, (src, dst) in enumerate(pairs)]
    for copy in copies:
        copy.start()
    tile = 256
    for h, (gate, up) in enumerate(((gate_b, up_b), (gate_v, up_v))):
        if h == 1:
            copies[0].wait()
            copies[1].wait()
        for j in range(0, half, tile):
            g = jnp.dot(rows[...], gate[:, j : j + tile], preferred_element_type=F32)
            u = jnp.dot(rows[...], up[:, j : j + tile], preferred_element_type=F32)
            hidden[:, h * half + j : h * half + j + tile] = (g / (1.0 + jnp.exp(-g)) * u).astype(BF)
    copies[2].wait()
    for c in range(0, width, tile):
        total = jnp.dot(hidden[:, :half], down_b[:, c : c + tile], preferred_element_type=F32)
        total = total + jnp.dot(hidden[:, half:], down_v[:, c : c + tile], preferred_element_type=F32)
        out[:, c : c + tile] = total.astype(BF)


def experts(rows, own, other):
    width, half = own[0].shape
    count = rows.shape[0]
    return pl.pallas_call(
        expert_kernel,
        out_shape=jax.ShapeDtypeStruct(rows.shape, BF),
        in_specs=[VMEM] + [pl.BlockSpec(memory_space=pl.ANY)] * 3 + [VMEM] * 3,
        out_specs=VMEM,
        scratch_shapes=[
            pltpu.VMEM((width, half), BF),
            pltpu.VMEM((width, half), BF),
            pltpu.VMEM((half, width), BF),
            pltpu.VMEM((count, 2 * half), BF),
            pltpu.SemaphoreType.DMA((3,)),
        ],
        compiler_params=pltpu.CompilerParams(vmem_limit_bytes=32 * MIB),
        cost_estimate=pl.CostEstimate(
            flops=2 * count * width * half * 6, bytes_accessed=12 * width * half + 4 * count * width, transcendentals=2 * count * half
        ),
        name="experts",
    )(rows, *own, *other)


def collect_kernel(returned, high, low, *outs):
    step = 512
    over = (((0,), (0,)), ((), ()))
    for c in range(0, returned.shape[1], step):
        part = returned[:, c : c + step]
        total = lax.dot_general(high[...], part, over, preferred_element_type=F32)
        total = total + lax.dot_general(low[...], part, over, preferred_element_type=F32)
        start = 0
        for out in outs:
            count = out.shape[0]
            out[:, c : c + step] = total[start : start + count].astype(out.dtype)
            start += count


def collect(returned, high, low, shapes):
    slots, width = returned.shape
    rows = high.shape[1]
    return pl.pallas_call(
        collect_kernel,
        out_shape=[jax.ShapeDtypeStruct((count, width), kind) for count, kind in shapes],
        compiler_params=pltpu.CompilerParams(vmem_limit_bytes=16 * MIB),
        cost_estimate=pl.CostEstimate(flops=4 * slots * rows * width, bytes_accessed=2 * (slots + rows) * width, transcendentals=0),
        name="collect",
    )(returned, high, low)


def groups():
    out = []
    for s in range(Z):
        for c in range(C):
            chips = [(p, y, x) for x in range(X) for p in range(PAIR) for y in range(Y)]
            if c == 1:
                chips = chips[::-1]
            out.append([(((s * PAIR + p) * Y + y) * X + x) * C + c for p, y, x in chips])
    return out


def exchange(value):
    width = value.shape[1]
    blocks = value.reshape(PLANE, -1, width)
    names = ("s", "p", "y", "x", "c")
    return lax.all_to_all(blocks, names, 0, 0, axis_index_groups=groups(), tiled=True).reshape(-1, width)


def body(tokens, expert_ids, gates, gate_weight, up_weight, down_weight):
    block, width = tokens.shape
    own_weights = [gate_weight[0], up_weight[0], down_weight[0]]
    own = extend(tokens, expert_ids, gates)
    other, sent_weights = lax.optimization_barrier((swap(own), own_weights[2:]))
    other_weights = [swap(w) for w in own_weights[:2] + sent_weights]
    own_weights[1:] = [pltpu.with_memory_space_constraint(w, pltpu.HBM) for w in own_weights[1:]]

    both = jnp.concatenate([own, other], axis=0)
    far = send(own, 2)
    near = send(both, 1)
    rows, high, low = place((both, near, far), block, width)
    rows, other_weights = lax.optimization_barrier((rows, other_weights))
    other_weights = [pltpu.with_memory_space_constraint(w, pltpu.VMEM) for w in other_weights]
    done = experts(exchange(rows), own_weights, other_weights)
    returned = exchange(done)
    shapes = ((block, F32), (block, F32), (block, BF), (block, BF))
    q_own, q_near, q_near_other, q_far = collect(returned, high, low, shapes)
    far = send(q_far, -1)
    near_other = back_across(q_near_other, 1)
    near = send((q_near + far.astype(F32)).astype(BF), -1)
    return (q_own + near_other.astype(F32) + near.astype(F32)).astype(BF)


def solution(mesh):
    names = ("s", "p", "y", "x", "c")
    fine = Mesh(mesh.devices.reshape(Z, PAIR, Y, X, C), names)
    rows = P(names)
    return jax.shard_map(body, mesh=fine, in_specs=(rows,) * 6, out_specs=rows, check_vma=False)
```
